32 devices in a mesh: wide: 8 (over z, core), narrow: 4 (over y, x).
Axes of the slice: x: 2, y: 2, z: 4, core: 2. Of those that a mesh axis runs over, the one named last changes fastest.
Arguments:
- rhs_panels: float32 [2, 1024, 4096], P(None, 'narrow', 'wide'), may hold values from -6 to 6
- rhs_rest: float32 [12288, 4096], P('narrow', 'wide'), may hold values from -6 to 6
- diag_inv: float32 [8, 1024, 1024], P('wide', 'narrow'), as said below
- couple: float32 [8, 1024, 1024], P('wide', 'narrow'), may hold values from -0.1875 to 0.1875
- off_blocks: float32 [8, 6144, 1024], P('wide', 'narrow'), may hold values from -0.1875 to 0.1875
- pattern: int32 [2, 24], P(None, 'narrow'), may hold values from 0 to 47, as said below
- owner: int32 [2], replicated, may hold values from 0 to 7, as said below
Outputs:
- solved: float32 [2, 1024, 4096], P(None, 'narrow', 'wide')
- rest_out: float32 [12288, 4096], P('narrow', 'wide')
The draws below stay inside these ranges and needn't reach their ends.
Inputs may be any that keep to these rules, and one draw needn't show every extreme that they name: `pattern`: entries j * 6 to (j + 1) * 6 - 1 of each row are 6 different increasing block numbers among j * 12 to (j + 1) * 12 - 1. `owner`: two different slots, one of them slot 7. `diag_inv`: each slot is lower triangular with a nonzero diagonal.
All inputs are finite; a program needn't handle non-finite values.
Results may differ from the reference program's by a relative error of at most 0.00012.
Values sent between devices are 32-bit elements; how exact they have to be, the bound alone decides.
A program may use at most 128 MiB of HBM per device.

```python
import jax
import jax.numpy as jnp
from jax import lax

PW = 1024
BLK = 256
REST_BLK = 12
OFF_DEV = 6
SLOTS = 8
NRHS = 4096
OFF = 24
REST = 12288


def draw_diag_inv(key, part):
    key_low = jax.random.fold_in(key, 11)
    key_diag = jax.random.fold_in(key, 12)
    row_ids = lax.broadcasted_iota(jnp.int32, (PW, PW), 0)
    col_ids = lax.broadcasted_iota(jnp.int32, (PW, PW), 1)
    lower = jax.random.normal(key_low, (SLOTS, PW, PW), jnp.float32) * (0.9 * PW ** (-0.5))
    diagonal = jax.random.uniform(key_diag, (SLOTS, PW, PW), jnp.float32, 0.6, 1.4)
    strict = (row_ids > col_ids)[None, :, :]
    onto = (row_ids == col_ids)[None, :, :]
    return jnp.where(strict, lower, 0.0) + jnp.where(onto, diagonal, 0.0)


def draw_pattern(key, part):
    groups = OFF // OFF_DEV
    keys = jax.random.split(jax.random.fold_in(key, 21), 2 * groups)
    picks = jax.vmap(lambda single: jnp.sort(jax.random.permutation(single, REST_BLK)[:OFF_DEV]))(keys)
    offsets = jnp.arange(2 * groups, dtype=jnp.int32) % groups * REST_BLK
    return (picks.astype(jnp.int32) + offsets[:, None]).reshape(2, OFF)


def draw_owner(key, part):
    key = jax.random.fold_in(key, 31)
    key_other = jax.random.fold_in(key, 1)
    key_side = jax.random.fold_in(key, 2)
    other = jax.random.randint(key_other, (), 0, SLOTS - 1, dtype=jnp.int32)
    side = jax.random.randint(key_side, (), 0, 2, dtype=jnp.int32)
    last = jnp.int32(SLOTS - 1)
    first_slot = jnp.where(side == 0, last, other)
    second_slot = jnp.where(side == 0, other, last)
    return jnp.stack([first_slot, second_slot]).astype(jnp.int32)


def block_levels(rng, shape, pieces, smallest, largest):
    loudness = 1.0
    for dim, blocks in pieces:
        heights = jax.random.uniform(jax.random.fold_in(jax.random.fold_in(rng, 6), dim), (blocks,), jnp.float32, smallest / len(pieces), largest / len(pieces))
        loudness = loudness * jnp.repeat(jnp.exp(heights), shape[dim] // blocks).reshape((-1,) + (1,) * (len(shape) - 1 - dim))
    return loudness


def normal_values(stream_key, extent, deviation, bound, cuts=(), held_as=jnp.bfloat16):
    values = deviation * jax.random.normal(stream_key, extent, jnp.float32)
    if cuts:
        values = values * block_levels(stream_key, extent, cuts, -0.22, 0.18)
    return jnp.clip(values, -bound, bound).astype(held_as)


def setup_inputs(seed: int = 0) -> dict:
    arg_keys = jax.random.split(jax.random.key(seed), 8)
    rhs_panels = normal_values(arg_keys[0], (2, PW, NRHS), 1.0, 6.0, ((1, 4), (2, 8)), jnp.float32)
    rhs_rest = normal_values(arg_keys[1], (REST, NRHS), 1.0, 6.0, ((0, 4), (1, 8)), jnp.float32)
    diag_inv = draw_diag_inv(jax.random.fold_in(arg_keys[7], 71), 0)
    couple = normal_values(arg_keys[3], (SLOTS, PW, PW), PW ** -0.5, 0.1875, ((0, 8), (1, 4)), jnp.float32)
    off_blocks = normal_values(arg_keys[4], (SLOTS, OFF * BLK, PW), PW ** -0.5, 0.1875, ((0, 8), (1, 4)), jnp.float32)
    pattern = draw_pattern(jax.random.fold_in(arg_keys[7], 71), 0)
    owner = draw_owner(jax.random.fold_in(arg_keys[7], 71), 0)
    return dict(rhs_panels=rhs_panels, rhs_rest=rhs_rest, diag_inv=diag_inv, couple=couple, off_blocks=off_blocks, pattern=pattern, owner=owner)


def matmul(left, right):
    return jnp.dot(left, right, preferred_element_type=jnp.float32, precision=lax.Precision.HIGHEST)


def apply_panel(remainder, off_rows, unknowns, indices):
    updates = matmul(off_rows, unknowns).reshape(-1, BLK, unknowns.shape[1])
    blocked = remainder.reshape(-1, BLK, remainder.shape[1])
    blocked = blocked.at[indices.astype(jnp.int32)].add(-updates)
    return blocked.reshape(remainder.shape)


def reference(rhs_panels, rhs_rest, diag_inv, couple, off_blocks, pattern, owner):
    first = matmul(diag_inv[owner[0]], rhs_panels[0])
    second_rhs = rhs_panels[1] - matmul(couple[owner[0]], first)
    second = matmul(diag_inv[owner[1]], second_rhs)
    remainder = apply_panel(rhs_rest, off_blocks[owner[0]], first, pattern[0])
    remainder = apply_panel(remainder, off_blocks[owner[1]], second, pattern[1])
    return jnp.stack([first, second]), remainder
```

```python
import functools

import jax
import jax.numpy as jnp
from jax import lax
from jax.experimental import pallas as pl
from jax.experimental.pallas import tpu as pltpu
from jax.sharding import PartitionSpec as P

BLK = 256
CH = 32
SKEW = 2
GROUP = 4
GAP = 10


def split(value):
    high = value.astype(jnp.bfloat16)
    low = (value - high.astype(jnp.float32)).astype(jnp.bfloat16)
    return high, low


def dot3(left, high, low):
    left_high, left_low = split(left)
    dot = functools.partial(jnp.dot, preferred_element_type=jnp.float32)
    return dot(left_high, high) + (dot(left_high, low) + dot(left_low, high))


def panels_kernel(
    pairs, narrow, owner_ref, rhs_ref, diag_ref, couple_ref, off_ref, solved_ref, u_ref,
    mine, sib, up, dn, other, full, xh, xl,
    load_sem, sib_send, sib_recv, up_send, up_recv, dn_send, dn_recv,
    pair_send, pair_recv, row_send, row_recv,
):
    wide = lax.axis_index("wide")
    row = lax.axis_index("narrow")
    pair = wide // 2
    half = wide % 2
    rows = diag_ref.shape[1]
    off_rows = off_ref.shape[1]
    depth = diag_ref.shape[2]
    part = rows // 2
    off_part = off_rows // 2
    nd = part // CH
    no = off_part // CH
    chunks = 3 * nd + 2 * no
    groups = no // GROUP

    def at(w, r):
        return dict(device_id=(w, r), device_id_type=pl.DeviceIdType.MESH)

    sibling = wide + 1 - 2 * half
    barrier = pltpu.get_barrier_semaphore()
    pl.semaphore_signal(barrier, inc=1, **at(sibling, row))
    for d in range(1, narrow):
        pl.semaphore_signal(barrier, inc=1, **at(wide, (row + d) % narrow))

    @pl.when(pair > 0)
    def _():
        pl.semaphore_signal(barrier, inc=1, **at(wide - 2, row))

    @pl.when(pair < pairs - 1)
    def _():
        pl.semaphore_signal(barrier, inc=1, **at(wide + 2, row))

    sources = ((diag_ref, 0, part), (couple_ref, part, part), (off_ref, 2 * part, off_part))

    def load(i):
        ref, base, size = sources[i]
        return pltpu.make_async_copy(
            ref.at[0, pl.ds(half * size, size)], mine.at[pl.ds(base, size)], load_sem.at[i]
        )

    def give(i):
        ref, base, size = sources[i]
        return pltpu.make_async_remote_copy(
            src_ref=ref.at[0, pl.ds((1 - half) * size, size)],
            dst_ref=sib.at[pl.ds(base, size)],
            send_sem=sib_send.at[i], recv_sem=sib_recv.at[i], **at(sibling, row),
        )

    for i in range(3):
        load(i).start()
    inner = (pair > 0) & (pair < pairs - 1)

    @pl.when(inner)
    def _():
        pl.semaphore_wait(barrier, narrow + 2)

    @pl.when(jnp.logical_not(inner))
    def _():
        pl.semaphore_wait(barrier, narrow + 1)

    for i in range(3):
        give(i).start()

    def gather(stage, d):
        here = full.at[stage, pl.ds(row * rows, rows)]
        return pltpu.make_async_remote_copy(
            src_ref=here, dst_ref=here,
            send_sem=row_send.at[stage, d - 1], recv_sem=row_recv.at[stage, d - 1],
            **at(wide, (row + d) % narrow),
        )

    def send_rows(stage, value):
        full[stage, pl.ds(row * rows, rows)] = value
        for d in range(1, narrow):
            gather(stage, d).start()

    def gathered(stage, slot):
        for d in range(1, narrow):
            came = full.at[stage, pl.ds((row + narrow - d) % narrow * rows, rows)]
            pltpu.make_async_remote_copy(
                src_ref=came, dst_ref=came,
                send_sem=row_send.at[stage, d - 1], recv_sem=row_recv.at[stage, d - 1],
                **at(wide, (row + d) % narrow),
            ).wait_recv()
        for d in range(1, narrow):
            gather(stage, d).wait_send()
        high, low = split(full[stage])
        xh[slot] = high
        xl[slot] = low

    send_rows(0, rhs_ref[0])
    for i in range(2):
        load(i).wait()
        give(i).wait()

    def mask(scalar):
        return jnp.full((CH, depth), scalar, jnp.int32) == 0

    segments = (
        (0, 0, nd, 0),
        (0, nd, nd, part),
        (1, 2 * nd, nd, 0),
        (0, 3 * nd, no, 2 * part),
        (1, 3 * nd + no, no, 2 * part),
    )

    def hop(k, step, buf, send_sem, recv_sem):
        return pltpu.make_async_remote_copy(
            src_ref=buf.at[k], dst_ref=buf.at[k],
            send_sem=send_sem.at[k], recv_sem=recv_sem.at[k], **at(wide + 2 * step, row),
        )

    def relay(k, step, buf, send_sem, recv_sem, has_in, has_out):
        for stream, start, count, base in segments:

            @pl.when((k >= start) & (k < start + count))
            def _():
                held = owner_ref[stream]
                window = pl.ds(base + (k - start) * CH, CH)

                @pl.when(has_in)
                def _():
                    hop(k, step, buf, send_sem, recv_sem).wait_recv()
                    value = jnp.where(mask(held - sibling), sib[window], buf[k])
                    buf[k] = jnp.where(mask(held - wide), mine[window], value)

                @pl.when(jnp.logical_not(has_in))
                def _():
                    buf[k] = jnp.where(mask(held - wide), mine[window], sib[window])

                @pl.when(has_out)
                def _():
                    hop(k, step, buf, send_sem, recv_sem).start()

    def share(k):
        return pltpu.make_async_remote_copy(
            src_ref=dn.at[k], dst_ref=other.at[k],
            send_sem=pair_send.at[k], recv_sem=pair_recv.at[k], **at(sibling, row),
        )

    def finish(k):
        @pl.when(pair < pairs - 1)
        def _():
            hop(k, 1, up, up_send, up_recv).wait_send()

        @pl.when(pair > 0)
        def _():
            hop(k, -1, dn, dn_send, dn_recv).wait_send()

        for stream, start, count, _base in segments:

            @pl.when((k >= start) & (k < start + count))
            def _():
                above = jnp.full((CH, depth), owner_ref[stream] // 2 - pair, jnp.int32) > 0
                dn[k] = jnp.where(above, dn[k], up[k])
                share(k).start()

    def landed(first, count):
        def wait(i, carry):
            share(first + i).wait()
            return carry

        lax.fori_loop(0, count, wait, 0)

    def rows_of(first, slot):
        landed(first, nd)
        own = dot3(dn[pl.ds(first, nd)].reshape(part, depth), xh[slot], xl[slot])
        far = dot3(other[pl.ds(first, nd)].reshape(part, depth), xh[slot], xl[slot])
        return own, far

    def put(ref, own, far):
        ref[pl.ds(half * part, part)] = own
        ref[pl.ds((1 - half) * part, part)] = far

    def update(stream, group):
        first = 3 * nd + stream * no + group * GROUP
        size = GROUP * CH
        landed(first, GROUP)
        own = dot3(dn[pl.ds(first, GROUP)].reshape(size, depth), xh[stream], xl[stream])
        u_ref[stream, pl.ds(half * off_part + group * size, size)] = own
        far = dot3(other[pl.ds(first, GROUP)].reshape(size, depth), xh[stream], xl[stream])
        u_ref[stream, pl.ds((1 - half) * off_part + group * size, size)] = far

    lag = SKEW * pairs
    first_at = max(3 * nd + GROUP, nd + GAP + 1)
    second_at = 3 * nd + no + GROUP

    def body(t, carry):
        @pl.when(t == 3 * nd)
        def _():
            load(2).wait()
            give(2).wait()

        relay(t - SKEW * pair, 1, up, up_send, up_recv, pair > 0, pair < pairs - 1)
        relay(
            t - SKEW * (pairs - 1 - pair), -1, dn, dn_send, dn_recv, pair < pairs - 1, pair > 0
        )
        f = t - lag

        @pl.when((f >= 0) & (f < chunks))
        def _():
            finish(f)

        @pl.when(f == nd)
        def _():
            gathered(0, 1)
            put(solved_ref.at[0], *rows_of(0, 1))
            send_rows(1, solved_ref[0])

        @pl.when(f == nd + GAP)
        def _():
            gathered(1, 0)
            put(solved_ref.at[1], *rows_of(nd, 0))
            send_rows(2, rhs_ref[1] - solved_ref[1])

        @pl.when(f == nd + 2 * GAP)
        def _():
            gathered(2, 1)
            put(solved_ref.at[1], *rows_of(2 * nd, 1))
            send_rows(3, solved_ref[1])

        g = f - first_at

        @pl.when((g >= 0) & (g < no) & (g % GROUP == 0))
        def _():
            update(0, g // GROUP)

        @pl.when(f == second_at)
        def _():
            gathered(3, 1)

        s = f - second_at

        @pl.when((s >= 0) & (s < no) & (s % GROUP == 0))
        def _():
            update(1, s // GROUP)

        return carry

    lax.fori_loop(0, lag + chunks + 1, body, 0)


def subtract_kernel(pattern_ref, rest_ref, first_ref, second_ref, out_ref):
    b = pl.program_id(0)
    count = pattern_ref.shape[1]
    total = rest_ref[...]
    for stream, ref in enumerate((first_ref, second_ref)):
        found = jnp.int32(0)
        for o in range(count):
            found = found + jnp.where(pattern_ref[stream, o] == b, 1, 0)
        hit = jnp.full(total.shape, found, jnp.int32) > 0
        total = total - jnp.where(hit, ref[0], 0.0)
    out_ref[...] = total


def per_device(pairs, narrow, rhs_panels, rhs_rest, diag_inv, couple, off_blocks, pattern, owner):
    _, rows, width = rhs_panels.shape
    depth = rows * narrow
    off_rows = off_blocks.shape[1]
    stack = rows + off_rows // 2
    chunks = (3 * rows + 2 * off_rows) // 2 // CH
    dma = pltpu.SemaphoreType.DMA
    vmem = pl.BlockSpec(memory_space=pltpu.VMEM)
    hbm = pl.BlockSpec(memory_space=pl.ANY)
    solved, updates = pl.pallas_call(
        functools.partial(panels_kernel, pairs, narrow),
        out_shape=(
            jax.ShapeDtypeStruct((2, rows, width), jnp.float32),
            jax.ShapeDtypeStruct((2, off_rows, width), jnp.float32),
        ),
        in_specs=[pl.BlockSpec(memory_space=pltpu.SMEM), vmem, hbm, hbm, hbm],
        out_specs=(vmem, vmem),
        scratch_shapes=[
            pltpu.VMEM((stack, depth), jnp.float32),
            pltpu.VMEM((stack, depth), jnp.float32),
            pltpu.VMEM((chunks, CH, depth), jnp.float32),
            pltpu.VMEM((chunks, CH, depth), jnp.float32),
            pltpu.VMEM((chunks, CH, depth), jnp.float32),
            pltpu.VMEM((4, depth, width), jnp.float32),
            pltpu.VMEM((2, depth, width), jnp.bfloat16),
            pltpu.VMEM((2, depth, width), jnp.bfloat16),
            dma((3,)),
            dma((3,)),
            dma((3,)),
            dma((chunks,)),
            dma((chunks,)),
            dma((chunks,)),
            dma((chunks,)),
            dma((chunks,)),
            dma((chunks,)),
            dma((4, narrow - 1)),
            dma((4, narrow - 1)),
        ],
        compiler_params=pltpu.CompilerParams(
            collective_id=0, has_side_effects=True, vmem_limit_bytes=60 * 2**20
        ),
        name="panels",
    )(owner, rhs_panels, diag_inv, couple, off_blocks)

    blocks = rhs_rest.shape[0] // BLK
    local = pattern - lax.axis_index("narrow") * blocks

    def place(stream):
        def index(b, pattern_ref):
            spot = jnp.int32(0)
            for o in range(pattern.shape[1]):
                spot = spot + jnp.where(pattern_ref[stream, o] == b, o, 0)
            return (stream, spot, 0)

        return index

    block = pl.BlockSpec((BLK, width), lambda b, pattern_ref: (b, 0))
    rest_out = pl.pallas_call(
        subtract_kernel,
        out_shape=jax.ShapeDtypeStruct(rhs_rest.shape, jnp.float32),
        grid_spec=pltpu.PrefetchScalarGridSpec(
            num_scalar_prefetch=1,
            grid=(blocks,),
            in_specs=[
                block,
                pl.BlockSpec((1, BLK, width), place(0)),
                pl.BlockSpec((1, BLK, width), place(1)),
            ],
            out_specs=block,
        ),
        name="subtract",
    )(local, rhs_rest, updates, updates)
    return solved, rest_out


def solution(mesh):
    in_specs = (
        P(None, "narrow", "wide"),
        P("narrow", "wide"),
        P("wide", "narrow", None),
        P("wide", "narrow", None),
        P("wide", "narrow", None),
        P(None, "narrow"),
        P(),
    )
    out_specs = (P(None, "narrow", "wide"), P("narrow", "wide"))
    step = functools.partial(per_device, mesh.shape["wide"] // 2, mesh.shape["narrow"])
    return jax.shard_map(
        step, mesh=mesh, in_specs=in_specs, out_specs=out_specs, check_vma=False
    )
```

```python
import functools

import jax
import jax.numpy as jnp
from jax import lax
from jax.experimental import pallas as pl
from jax.experimental.pallas import tpu as pltpu
from jax.sharding import PartitionSpec as P

BLK = 256
CH = 32
SKEW = 4
GROUP = 4
GAP = 10


def split(value):
    high = value.astype(jnp.bfloat16)
    low = (value - high.astype(jnp.float32)).astype(jnp.bfloat16)
    return high, low


def dot3(left, high, low):
    left_high, left_low = split(left)
    dot = functools.partial(jnp.dot, preferred_element_type=jnp.float32)
    return dot(left_high, high) + (dot(left_high, low) + dot(left_low, high))


def panels_kernel(
    pairs, narrow, owner_ref, rhs_ref, diag_ref, couple_ref, off_ref, solved_ref, u_ref,
    mine, sib, up, dn, other, full, xh, xl,
    load_sem, sib_send, sib_recv, up_send, up_recv, dn_send, dn_recv,
    pair_send, pair_recv, row_send, row_recv,
):
    wide = lax.axis_index("wide")
    row = lax.axis_index("narrow")
    pair = wide // 2
    half = wide % 2
    rows = diag_ref.shape[1]
    off_rows = off_ref.shape[1]
    depth = diag_ref.shape[2]
    part = rows // 2
    off_part = off_rows // 2
    nd = part // CH
    no = off_part // CH
    chunks = 3 * nd + 2 * no
    groups = no // GROUP

    def at(w, r):
        return dict(device_id=(w, r), device_id_type=pl.DeviceIdType.MESH)

    sibling = wide + 1 - 2 * half
    barrier = pltpu.get_barrier_semaphore()
    pl.semaphore_signal(barrier, inc=1, **at(sibling, row))
    for d in range(1, narrow):
        pl.semaphore_signal(barrier, inc=1, **at(wide, (row + d) % narrow))

    @pl.when(pair > 0)
    def _():
        pl.semaphore_signal(barrier, inc=1, **at(wide - 2, row))

    @pl.when(pair < pairs - 1)
    def _():
        pl.semaphore_signal(barrier, inc=1, **at(wide + 2, row))

    sources = ((diag_ref, 0, part), (couple_ref, part, part), (off_ref, 2 * part, off_part))

    def load(i):
        ref, base, size = sources[i]
        return pltpu.make_async_copy(
            ref.at[0, pl.ds(half * size, size)], mine.at[pl.ds(base, size)], load_sem.at[i]
        )

    def give(i):
        ref, base, size = sources[i]
        return pltpu.make_async_remote_copy(
            src_ref=ref.at[0, pl.ds((1 - half) * size, size)],
            dst_ref=sib.at[pl.ds(base, size)],
            send_sem=sib_send.at[i], recv_sem=sib_recv.at[i], **at(sibling, row),
        )

    for i in range(3):
        load(i).start()
    inner = (pair > 0) & (pair < pairs - 1)

    @pl.when(inner)
    def _():
        pl.semaphore_wait(barrier, narrow + 2)

    @pl.when(jnp.logical_not(inner))
    def _():
        pl.semaphore_wait(barrier, narrow + 1)

    for i in range(3):
        give(i).start()

    def gather(stage, d):
        here = full.at[stage, pl.ds(row * rows, rows)]
        return pltpu.make_async_remote_copy(
            src_ref=here, dst_ref=here,
            send_sem=row_send.at[stage, d - 1], recv_sem=row_recv.at[stage, d - 1],
            **at(wide, (row + d) % narrow),
        )

    def send_rows(stage, value):
        full[stage, pl.ds(row * rows, rows)] = value
        for d in range(1, narrow):
            gather(stage, d).start()

    def gathered(stage, slot):
        for d in range(1, narrow):
            came = full.at[stage, pl.ds((row + narrow - d) % narrow * rows, rows)]
            pltpu.make_async_remote_copy(
                src_ref=came, dst_ref=came,
                send_sem=row_send.at[stage, d - 1], recv_sem=row_recv.at[stage, d - 1],
                **at(wide, (row + d) % narrow),
            ).wait_recv()
        for d in range(1, narrow):
            gather(stage, d).wait_send()
        high, low = split(full[stage])
        xh[slot] = high
        xl[slot] = low

    send_rows(0, rhs_ref[0])
    for i in range(2):
        load(i).wait()
        give(i).wait()

    def mask(scalar):
        return jnp.full((CH, depth), scalar, jnp.int32) == 0

    segments = (
        (0, 0, nd, 0),
        (0, nd, nd, part),
        (1, 2 * nd, nd, 0),
        (0, 3 * nd, no, 2 * part),
        (1, 3 * nd + no, no, 2 * part),
    )

    def hop(k, step, buf, send_sem, recv_sem):
        return pltpu.make_async_remote_copy(
            src_ref=buf.at[k], dst_ref=buf.at[k],
            send_sem=send_sem.at[k], recv_sem=recv_sem.at[k], **at(wide + 2 * step, row),
        )

    def relay(k, step, buf, send_sem, recv_sem, has_in, has_out):
        for stream, start, count, base in segments:

            @pl.when((k >= start) & (k < start + count))
            def _():
                held = owner_ref[stream]
                window = pl.ds(base + (k - start) * CH, CH)

                @pl.when(has_in)
                def _():
                    hop(k, step, buf, send_sem, recv_sem).wait_recv()
                    value = jnp.where(mask(held - sibling), sib[window], buf[k])
                    buf[k] = jnp.where(mask(held - wide), mine[window], value)

                @pl.when(jnp.logical_not(has_in))
                def _():
                    buf[k] = jnp.where(mask(held - wide), mine[window], sib[window])

                @pl.when(has_out)
                def _():
                    hop(k, step, buf, send_sem, recv_sem).start()

    def share(k):
        return pltpu.make_async_remote_copy(
            src_ref=dn.at[k], dst_ref=other.at[k],
            send_sem=pair_send.at[k], recv_sem=pair_recv.at[k], **at(sibling, row),
        )

    def finish(k):
        @pl.when(pair < pairs - 1)
        def _():
            hop(k, 1, up, up_send, up_recv).wait_send()

        @pl.when(pair > 0)
        def _():
            hop(k, -1, dn, dn_send, dn_recv).wait_send()

        for stream, start, count, _base in segments:

            @pl.when((k >= start) & (k < start + count))
            def _():
                above = jnp.full((CH, depth), owner_ref[stream] // 2 - pair, jnp.int32) > 0
                dn[k] = jnp.where(above, dn[k], up[k])
                share(k).start()

    def landed(first, count):
        def wait(i, carry):
            share(first + i).wait()
            return carry

        lax.fori_loop(0, count, wait, 0)

    def rows_of(first, slot):
        landed(first, nd)
        own = dot3(dn[pl.ds(first, nd)].reshape(part, depth), xh[slot], xl[slot])
        far = dot3(other[pl.ds(first, nd)].reshape(part, depth), xh[slot], xl[slot])
        return own, far

    def put(ref, own, far):
        ref[pl.ds(half * part, part)] = own
        ref[pl.ds((1 - half) * part, part)] = far

    def update(stream, group):
        first = 3 * nd + stream * no + group * GROUP
        size = GROUP * CH
        landed(first, GROUP)
        own = dot3(dn[pl.ds(first, GROUP)].reshape(size, depth), xh[stream], xl[stream])
        u_ref[stream, pl.ds(half * off_part + group * size, size)] = own
        far = dot3(other[pl.ds(first, GROUP)].reshape(size, depth), xh[stream], xl[stream])
        u_ref[stream, pl.ds((1 - half) * off_part + group * size, size)] = far

    lag = SKEW * (pairs - 1) + 1
    first_at = max(3 * nd + GROUP, nd + GAP + 1)
    second_at = 3 * nd + no + GROUP

    def body(t, carry):
        @pl.when(t == 3 * nd)
        def _():
            load(2).wait()
            give(2).wait()

        relay(t - SKEW * pair, 1, up, up_send, up_recv, pair > 0, pair < pairs - 1)
        relay(
            t - SKEW * (pairs - 1 - pair), -1, dn, dn_send, dn_recv, pair < pairs - 1, pair > 0
        )
        f = t - lag

        @pl.when((f >= 0) & (f < chunks))
        def _():
            finish(f)

        @pl.when(f == nd)
        def _():
            gathered(0, 1)
            put(solved_ref.at[0], *rows_of(0, 1))
            send_rows(1, solved_ref[0])

        @pl.when(f == nd + GAP)
        def _():
            gathered(1, 0)
            put(solved_ref.at[1], *rows_of(nd, 0))
            send_rows(2, rhs_ref[1] - solved_ref[1])

        @pl.when(f == nd + 2 * GAP)
        def _():
            gathered(2, 1)
            put(solved_ref.at[1], *rows_of(2 * nd, 1))
            send_rows(3, solved_ref[1])

        g = f - first_at

        @pl.when((g >= 0) & (g < no) & (g % GROUP == 0))
        def _():
            update(0, g // GROUP)

        @pl.when(f == second_at)
        def _():
            gathered(3, 1)

        s = f - second_at

        @pl.when((s >= 0) & (s < no) & (s % GROUP == 0))
        def _():
            update(1, s // GROUP)

        return carry

    lax.fori_loop(0, lag + chunks + 1, body, 0)


def subtract_kernel(pattern_ref, rest_ref, first_ref, second_ref, out_ref):
    b = pl.program_id(0)
    count = pattern_ref.shape[1]
    total = rest_ref[...]
    for stream, ref in enumerate((first_ref, second_ref)):
        found = jnp.int32(0)
        for o in range(count):
            found = found + jnp.where(pattern_ref[stream, o] == b, 1, 0)
        hit = jnp.full(total.shape, found, jnp.int32) > 0
        total = total - jnp.where(hit, ref[0], 0.0)
    out_ref[...] = total


def per_device(pairs, narrow, rhs_panels, rhs_rest, diag_inv, couple, off_blocks, pattern, owner):
    _, rows, width = rhs_panels.shape
    depth = rows * narrow
    off_rows = off_blocks.shape[1]
    stack = rows + off_rows // 2
    chunks = (3 * rows + 2 * off_rows) // 2 // CH
    dma = pltpu.SemaphoreType.DMA
    vmem = pl.BlockSpec(memory_space=pltpu.VMEM)
    hbm = pl.BlockSpec(memory_space=pl.ANY)
    solved, updates = pl.pallas_call(
        functools.partial(panels_kernel, pairs, narrow),
        out_shape=(
            jax.ShapeDtypeStruct((2, rows, width), jnp.float32),
            jax.ShapeDtypeStruct((2, off_rows, width), jnp.float32),
        ),
        in_specs=[pl.BlockSpec(memory_space=pltpu.SMEM), vmem, hbm, hbm, hbm],
        out_specs=(vmem, vmem),
        scratch_shapes=[
            pltpu.VMEM((stack, depth), jnp.float32),
            pltpu.VMEM((stack, depth), jnp.float32),
            pltpu.VMEM((chunks, CH, depth), jnp.float32),
            pltpu.VMEM((chunks, CH, depth), jnp.float32),
            pltpu.VMEM((chunks, CH, depth), jnp.float32),
            pltpu.VMEM((4, depth, width), jnp.float32),
            pltpu.VMEM((2, depth, width), jnp.bfloat16),
            pltpu.VMEM((2, depth, width), jnp.bfloat16),
            dma((3,)),
            dma((3,)),
            dma((3,)),
            dma((chunks,)),
            dma((chunks,)),
            dma((chunks,)),
            dma((chunks,)),
            dma((chunks,)),
            dma((chunks,)),
            dma((4, narrow - 1)),
            dma((4, narrow - 1)),
        ],
        compiler_params=pltpu.CompilerParams(
            collective_id=0, has_side_effects=True, vmem_limit_bytes=60 * 2**20
        ),
        name="panels",
    )(owner, rhs_panels, diag_inv, couple, off_blocks)

    blocks = rhs_rest.shape[0] // BLK
    local = pattern - lax.axis_index("narrow") * blocks

    def place(stream):
        def index(b, pattern_ref):
            spot = jnp.int32(0)
            for o in range(pattern.shape[1]):
                spot = spot + jnp.where(pattern_ref[stream, o] <= b, 1, 0)
            return (stream, jnp.maximum(spot - 1, 0), 0)

        return index

    block = pl.BlockSpec((BLK, width), lambda b, pattern_ref: (b, 0))
    rest_out = pl.pallas_call(
        subtract_kernel,
        out_shape=jax.ShapeDtypeStruct(rhs_rest.shape, jnp.float32),
        grid_spec=pltpu.PrefetchScalarGridSpec(
            num_scalar_prefetch=1,
            grid=(blocks,),
            in_specs=[
                block,
                pl.BlockSpec((1, BLK, width), place(0)),
                pl.BlockSpec((1, BLK, width), place(1)),
            ],
            out_specs=block,
        ),
        name="subtract",
    )(local, rhs_rest, updates, updates)
    return solved, rest_out


def solution(mesh):
    in_specs = (
        P(None, "narrow", "wide"),
        P("narrow", "wide"),
        P("wide", "narrow", None),
        P("wide", "narrow", None),
        P("wide", "narrow", None),
        P(None, "narrow"),
        P(),
    )
    out_specs = (P(None, "narrow", "wide"), P("narrow", "wide"))
    step = functools.partial(per_device, mesh.shape["wide"] // 2, mesh.shape["narrow"])
    return jax.shard_map(
        step, mesh=mesh, in_specs=in_specs, out_specs=out_specs, check_vma=False
    )
```

```python
import functools

import jax
import jax.numpy as jnp
from jax import lax
from jax.experimental import pallas as pl
from jax.experimental.pallas import tpu as pltpu
from jax.sharding import PartitionSpec as P

BLK = 256
CH = 32
SKEW = 1
GROUP = 4
GAP = 10


def split(value):
    high = value.astype(jnp.bfloat16)
    low = (value - high.astype(jnp.float32)).astype(jnp.bfloat16)
    return high, low


def dot3(left, high, low):
    left_high, left_low = split(left)
    dot = functools.partial(jnp.dot, preferred_element_type=jnp.float32)
    return dot(left_high, high) + (dot(left_high, low) + dot(left_low, high))


def panels_kernel(
    pairs, narrow, owner_ref, rhs_ref, diag_ref, couple_ref, off_ref, solved_ref, u_ref,
    mine, sib, up, dn, other, full, xh, xl,
    load_sem, sib_send, sib_recv, up_send, up_recv, dn_send, dn_recv,
    pair_send, pair_recv, row_send, row_recv,
):
    wide = lax.axis_index("wide")
    row = lax.axis_index("narrow")
    pair = wide // 2
    half = wide % 2
    rows = diag_ref.shape[1]
    off_rows = off_ref.shape[1]
    depth = diag_ref.shape[2]
    part = rows // 2
    off_part = off_rows // 2
    nd = part // CH
    no = off_part // CH
    chunks = 3 * nd + 2 * no
    groups = no // GROUP

    def at(w, r):
        return dict(device_id=(w, r), device_id_type=pl.DeviceIdType.MESH)

    sibling = wide + 1 - 2 * half
    barrier = pltpu.get_barrier_semaphore()
    pl.semaphore_signal(barrier, inc=1, **at(sibling, row))
    for d in range(1, narrow):
        pl.semaphore_signal(barrier, inc=1, **at(wide, (row + d) % narrow))

    @pl.when(pair > 0)
    def _():
        pl.semaphore_signal(barrier, inc=1, **at(wide - 2, row))

    @pl.when(pair < pairs - 1)
    def _():
        pl.semaphore_signal(barrier, inc=1, **at(wide + 2, row))

    sources = ((diag_ref, 0, part), (couple_ref, part, part), (off_ref, 2 * part, off_part))

    def load(i):
        ref, base, size = sources[i]
        return pltpu.make_async_copy(
            ref.at[0, pl.ds(half * size, size)], mine.at[pl.ds(base, size)], load_sem.at[i]
        )

    def give(i):
        ref, base, size = sources[i]
        return pltpu.make_async_remote_copy(
            src_ref=ref.at[0, pl.ds((1 - half) * size, size)],
            dst_ref=sib.at[pl.ds(base, size)],
            send_sem=sib_send.at[i], recv_sem=sib_recv.at[i], **at(sibling, row),
        )

    for i in range(3):
        load(i).start()
    inner = (pair > 0) & (pair < pairs - 1)

    @pl.when(inner)
    def _():
        pl.semaphore_wait(barrier, narrow + 2)

    @pl.when(jnp.logical_not(inner))
    def _():
        pl.semaphore_wait(barrier, narrow + 1)

    for i in range(3):
        give(i).start()

    def gather(stage, d):
        here = full.at[stage, pl.ds(row * rows, rows)]
        return pltpu.make_async_remote_copy(
            src_ref=here, dst_ref=here,
            send_sem=row_send.at[stage, d - 1], recv_sem=row_recv.at[stage, d - 1],
            **at(wide, (row + d) % narrow),
        )

    def send_rows(stage, value):
        full[stage, pl.ds(row * rows, rows)] = value
        for d in range(1, narrow):
            gather(stage, d).start()

    def gathered(stage, slot):
        for d in range(1, narrow):
            came = full.at[stage, pl.ds((row + narrow - d) % narrow * rows, rows)]
            pltpu.make_async_remote_copy(
                src_ref=came, dst_ref=came,
                send_sem=row_send.at[stage, d - 1], recv_sem=row_recv.at[stage, d - 1],
                **at(wide, (row + d) % narrow),
            ).wait_recv()
        for d in range(1, narrow):
            gather(stage, d).wait_send()
        high, low = split(full[stage])
        xh[slot] = high
        xl[slot] = low

    send_rows(0, rhs_ref[0])
    for i in range(2):
        load(i).wait()
        give(i).wait()

    def mask(scalar):
        return jnp.full((CH, depth), scalar, jnp.int32) == 0

    segments = (
        (0, 0, nd, 0),
        (0, nd, nd, part),
        (1, 2 * nd, nd, 0),
        (0, 3 * nd, no, 2 * part),
        (1, 3 * nd + no, no, 2 * part),
    )

    def hop(k, step, buf, send_sem, recv_sem):
        return pltpu.make_async_remote_copy(
            src_ref=buf.at[k], dst_ref=buf.at[k],
            send_sem=send_sem.at[k], recv_sem=recv_sem.at[k], **at(wide + 2 * step, row),
        )

    def relay(k, step, buf, send_sem, recv_sem, has_in, has_out):
        for stream, start, count, base in segments:

            @pl.when((k >= start) & (k < start + count))
            def _():
                held = owner_ref[stream]
                window = pl.ds(base + (k - start) * CH, CH)

                @pl.when(has_in)
                def _():
                    hop(k, step, buf, send_sem, recv_sem).wait_recv()
                    value = jnp.where(mask(held - sibling), sib[window], buf[k])
                    buf[k] = jnp.where(mask(held - wide), mine[window], value)

                @pl.when(jnp.logical_not(has_in))
                def _():
                    buf[k] = jnp.where(mask(held - wide), mine[window], sib[window])

                @pl.when(has_out)
                def _():
                    hop(k, step, buf, send_sem, recv_sem).start()

    def share(k):
        return pltpu.make_async_remote_copy(
            src_ref=dn.at[k], dst_ref=other.at[k],
            send_sem=pair_send.at[k], recv_sem=pair_recv.at[k], **at(sibling, row),
        )

    def finish(k):
        @pl.when(pair < pairs - 1)
        def _():
            hop(k, 1, up, up_send, up_recv).wait_send()

        @pl.when(pair > 0)
        def _():
            hop(k, -1, dn, dn_send, dn_recv).wait_send()

        for stream, start, count, _base in segments:

            @pl.when((k >= start) & (k < start + count))
            def _():
                above = jnp.full((CH, depth), owner_ref[stream] // 2 - pair, jnp.int32) > 0
                dn[k] = jnp.where(above, dn[k], up[k])
                share(k).start()

    def landed(first, count):
        def wait(i, carry):
            share(first + i).wait()
            return carry

        lax.fori_loop(0, count, wait, 0)

    def rows_of(first, slot):
        landed(first, nd)
        own = dot3(dn[pl.ds(first, nd)].reshape(part, depth), xh[slot], xl[slot])
        far = dot3(other[pl.ds(first, nd)].reshape(part, depth), xh[slot], xl[slot])
        return own, far

    def put(ref, own, far):
        ref[pl.ds(half * part, part)] = own
        ref[pl.ds((1 - half) * part, part)] = far

    def update(stream, group):
        first = 3 * nd + stream * no + group * GROUP
        size = GROUP * CH
        landed(first, GROUP)
        own = dot3(dn[pl.ds(first, GROUP)].reshape(size, depth), xh[stream], xl[stream])
        u_ref[stream, pl.ds(half * off_part + group * size, size)] = own
        far = dot3(other[pl.ds(first, GROUP)].reshape(size, depth), xh[stream], xl[stream])
        u_ref[stream, pl.ds((1 - half) * off_part + group * size, size)] = far

    lag = SKEW * (pairs - 1) + 2
    first_at = max(3 * nd + GROUP, nd + GAP + 1)
    second_at = 3 * nd + no + GROUP

    def body(t, carry):
        @pl.when(t == 3 * nd)
        def _():
            load(2).wait()
            give(2).wait()

        relay(t - SKEW * pair, 1, up, up_send, up_recv, pair > 0, pair < pairs - 1)
        relay(
            t - SKEW * (pairs - 1 - pair), -1, dn, dn_send, dn_recv, pair < pairs - 1, pair > 0
        )
        f = t - lag

        @pl.when((f >= 0) & (f < chunks))
        def _():
            finish(f)

        @pl.when(f == nd)
        def _():
            gathered(0, 1)
            put(solved_ref.at[0], *rows_of(0, 1))
            send_rows(1, solved_ref[0])

        @pl.when(f == nd + GAP)
        def _():
            gathered(1, 0)
            put(solved_ref.at[1], *rows_of(nd, 0))
            send_rows(2, rhs_ref[1] - solved_ref[1])

        @pl.when(f == nd + 2 * GAP)
        def _():
            gathered(2, 1)
            put(solved_ref.at[1], *rows_of(2 * nd, 1))
            send_rows(3, solved_ref[1])

        g = f - first_at

        @pl.when((g >= 0) & (g < no) & (g % GROUP == 0))
        def _():
            update(0, g // GROUP)

        @pl.when(f == second_at)
        def _():
            gathered(3, 1)

        s = f - second_at

        @pl.when((s >= 0) & (s < no) & (s % GROUP == 0))
        def _():
            update(1, s // GROUP)

        return carry

    lax.fori_loop(0, lag + chunks + 1, body, 0)


def subtract_kernel(pattern_ref, rest_ref, first_ref, second_ref, out_ref):
    b = pl.program_id(0)
    count = pattern_ref.shape[1]
    total = rest_ref[...]
    for stream, ref in enumerate((first_ref, second_ref)):
        found = jnp.int32(0)
        for o in range(count):
            found = found + jnp.where(pattern_ref[stream, o] == b, 1, 0)
        hit = jnp.full(total.shape, found, jnp.int32) > 0
        total = total - jnp.where(hit, ref[0], 0.0)
    out_ref[...] = total


def per_device(pairs, narrow, rhs_panels, rhs_rest, diag_inv, couple, off_blocks, pattern, owner):
    _, rows, width = rhs_panels.shape
    depth = rows * narrow
    off_rows = off_blocks.shape[1]
    stack = rows + off_rows // 2
    chunks = (3 * rows + 2 * off_rows) // 2 // CH
    dma = pltpu.SemaphoreType.DMA
    vmem = pl.BlockSpec(memory_space=pltpu.VMEM)
    hbm = pl.BlockSpec(memory_space=pl.ANY)
    solved, updates = pl.pallas_call(
        functools.partial(panels_kernel, pairs, narrow),
        out_shape=(
            jax.ShapeDtypeStruct((2, rows, width), jnp.float32),
            jax.ShapeDtypeStruct((2, off_rows, width), jnp.float32),
        ),
        in_specs=[pl.BlockSpec(memory_space=pltpu.SMEM), vmem, hbm, hbm, hbm],
        out_specs=(vmem, vmem),
        scratch_shapes=[
            pltpu.VMEM((stack, depth), jnp.float32),
            pltpu.VMEM((stack, depth), jnp.float32),
            pltpu.VMEM((chunks, CH, depth), jnp.float32),
            pltpu.VMEM((chunks, CH, depth), jnp.float32),
            pltpu.VMEM((chunks, CH, depth), jnp.float32),
            pltpu.VMEM((4, depth, width), jnp.float32),
            pltpu.VMEM((2, depth, width), jnp.bfloat16),
            pltpu.VMEM((2, depth, width), jnp.bfloat16),
            dma((3,)),
            dma((3,)),
            dma((3,)),
            dma((chunks,)),
            dma((chunks,)),
            dma((chunks,)),
            dma((chunks,)),
            dma((chunks,)),
            dma((chunks,)),
            dma((4, narrow - 1)),
            dma((4, narrow - 1)),
        ],
        compiler_params=pltpu.CompilerParams(
            collective_id=0, has_side_effects=True, vmem_limit_bytes=60 * 2**20
        ),
        name="panels",
    )(owner, rhs_panels, diag_inv, couple, off_blocks)

    blocks = rhs_rest.shape[0] // BLK
    local = pattern - lax.axis_index("narrow") * blocks

    def place(stream):
        def index(b, pattern_ref):
            spot = jnp.int32(0)
            for o in range(pattern.shape[1]):
                spot = spot + jnp.where(pattern_ref[stream, o] == b, o, 0)
            return (stream, spot, 0)

        return index

    block = pl.BlockSpec((BLK, width), lambda b, pattern_ref: (b, 0))
    rest_out = pl.pallas_call(
        subtract_kernel,
        out_shape=jax.ShapeDtypeStruct(rhs_rest.shape, jnp.float32),
        grid_spec=pltpu.PrefetchScalarGridSpec(
            num_scalar_prefetch=1,
            grid=(blocks,),
            in_specs=[
                block,
                pl.BlockSpec((1, BLK, width), place(0)),
                pl.BlockSpec((1, BLK, width), place(1)),
            ],
            out_specs=block,
        ),
        name="subtract",
    )(local, rhs_rest, updates, updates)
    return solved, rest_out


def solution(mesh):
    in_specs = (
        P(None, "narrow", "wide"),
        P("narrow", "wide"),
        P("wide", "narrow", None),
        P("wide", "narrow", None),
        P("wide", "narrow", None),
        P(None, "narrow"),
        P(),
    )
    out_specs = (P(None, "narrow", "wide"), P("narrow", "wide"))
    step = functools.partial(per_device, mesh.shape["wide"] // 2, mesh.shape["narrow"])
    return jax.shard_map(
        step, mesh=mesh, in_specs=in_specs, out_specs=out_specs, check_vma=False
    )
```
